32 devices in a mesh: rows: 2 (over x), seq: 16 (over z, y, core).
Axes of the slice: x: 2, y: 2, z: 4, core: 2. Of those that a mesh axis runs over, the one named last changes fastest.
Arguments:
- states: bfloat16 [2, 2048, 512], P('rows', 'seq'), may hold values from -6 to 6
- memory: bfloat16 [2, 128, 512], P('rows', 'seq'), may hold values from -6 to 6
- target_segments: int32 [2, 2048], P('rows', 'seq'), may hold values from 0 to 2, as said below
- memory_segments: int32 [2, 128], P('rows', 'seq'), may hold values from 0 to 2, as said below
- self_query: bfloat16 [512, 512], replicated, may hold values from -0.25 to 0.25
- self_key: bfloat16 [512, 512], replicated, may hold values from -0.25 to 0.25
- self_value: bfloat16 [512, 512], replicated, may hold values from -0.25 to 0.25
- self_out: bfloat16 [512, 512], replicated, may hold values from -1 to 1
- gain_one: float32 [512], replicated, may hold values from 0.25 to 1.75
- shift_one: float32 [512], replicated, may hold values from -1.5 to 1.5
- cross_query: bfloat16 [512, 512], replicated, may hold values from -0.25 to 0.25
- cross_key: bfloat16 [512, 512], replicated, may hold values from -0.25 to 0.25
- cross_value: bfloat16 [512, 512], replicated, may hold values from -0.25 to 0.25
- cross_out: bfloat16 [512, 512], replicated, may hold values from -1 to 1
- gain_two: float32 [512], replicated, may hold values from 0.25 to 1.75
- shift_two: float32 [512], replicated, may hold values from -1.5 to 1.5
- expand_weight: bfloat16 [512, 2048], replicated, may hold values from -0.25 to 0.25
- reduce_weight: bfloat16 [2048, 512], replicated, may hold values from -0.25 to 0.25
- gain_three: float32 [512], replicated, may hold values from 0.25 to 1.75
- shift_three: float32 [512], replicated, may hold values from -1.5 to 1.5
- output_cotangent: bfloat16 [2, 2048, 512], P('rows', 'seq'), may hold values from -6 to 6
Outputs:
- layer_output: bfloat16 [2, 2048, 512], P('rows', 'seq')
- states_grad: float32 [2, 2048, 512], P('rows', 'seq')
- memory_grad: float32 [2, 128, 512], P('rows', 'seq')
- self_query_grad: float32 [512, 512], replicated
- self_key_grad: float32 [512, 512], replicated
- self_value_grad: float32 [512, 512], replicated
- self_out_grad: float32 [512, 512], replicated
- gain_one_grad: float32 [512], replicated
- shift_one_grad: float32 [512], replicated
- cross_query_grad: float32 [512, 512], replicated
- cross_key_grad: float32 [512, 512], replicated
- cross_value_grad: float32 [512, 512], replicated
- cross_out_grad: float32 [512, 512], replicated
- gain_two_grad: float32 [512], replicated
- shift_two_grad: float32 [512], replicated
- expand_weight_grad: float32 [512, 2048], replicated
- reduce_weight_grad: float32 [2048, 512], replicated
- gain_three_grad: float32 [512], replicated
- shift_three_grad: float32 [512], replicated
The draws below stay inside these ranges and needn't reach their ends.
Inputs may be any that keep to these rules, and one draw needn't show every extreme that they name: `target_segments`: in each row the ids never fall and each of 0, 1, 2 holds at least one position; id 0 lies within the first 127 positions and id 2 within the last 127 positions. `memory_segments`: in each row the ids never fall and each of 0, 1, 2 holds at least one position; id 0 lies within the first 7 positions and id 2 within the last 7 positions.
All inputs are finite; a program needn't handle non-finite values.
Results may differ from the reference program's by a relative error of at most 0.04.
Values may be sent and summed in bfloat16 or wider, within the bound.
A program may use at most 320 MiB of HBM per device.

```python
import jax
import jax.numpy as jnp
from jax import lax

D = 512
HEADS = 8
HEAD_DIM = 64
FF = 2048
TOK_DEV = 128
MEM_DEV = 8
ROWS = 2
LEN = 2048
MLEN = 128


def three_pairs(key, width, length):
    head_key, tail_key = jax.random.split(key)
    head = jax.random.randint(head_key, (ROWS, 1), 1, width)
    tail = length - jax.random.randint(tail_key, (ROWS, 1), 1, width)
    places = jnp.arange(length, dtype=jnp.int32)[None, :]
    return (places >= head).astype(jnp.int32) + (places >= tail).astype(jnp.int32)


def draw_target_segments(key, part):
    key = jax.random.fold_in(key, 11)
    return three_pairs(key, TOK_DEV, LEN)


def draw_memory_segments(key, part):
    key = jax.random.fold_in(key, 12)
    return three_pairs(key, MEM_DEV, MLEN)


def block_scale(own_key, shape, cuts, smallest, high):
    level, own = 1.0, jax.random.fold_in(own_key, 6)
    for dim, blocks in cuts:
        heights = jnp.exp(jax.random.uniform(jax.random.fold_in(own, dim), (blocks,), jnp.float32, smallest / len(cuts), high / len(cuts)))
        level = level * jnp.repeat(heights, shape[dim] // blocks).reshape([-1 if axis == dim else 1 for axis in range(len(shape))])
    return level


def normal_values(rng, shape, scale, bound, shards=(), kind=jnp.bfloat16):
    level = block_scale(rng, shape, shards, -0.22, 0.18) if shards else 1.0
    array = jax.random.normal(rng, shape, jnp.float32) * scale * level
    return jnp.minimum(jnp.maximum(array, -bound), bound).astype(kind)


def setup_inputs(seed: int = 0) -> dict:
    streams_of = jax.random.split(jax.random.key(seed), 22)
    states = normal_values(streams_of[0], (ROWS, LEN, D), 1.0, 6.0, ((0, 2), (1, 16)))
    memory = normal_values(streams_of[1], (ROWS, MLEN, D), 1.0, 6.0, ((0, 2), (1, 16)))
    target_segments = draw_target_segments(jax.random.fold_in(streams_of[21], 71), 0)
    memory_segments = draw_memory_segments(jax.random.fold_in(streams_of[21], 71), 0)
    self_query = normal_values(streams_of[4], (D, D), D ** -0.5, 0.25)
    self_key = normal_values(streams_of[5], (D, D), D ** -0.5, 0.25)
    self_value = normal_values(streams_of[6], (D, D), D ** -0.5, 0.25)
    self_out = normal_values(streams_of[7], (D, D), (D // 16) ** -0.5, 1.0)
    gain_one = jnp.clip(1.0 + 0.15 * jax.random.normal(streams_of[8], (D,), jnp.float32), 0.25, 1.75)
    shift_one = normal_values(streams_of[9], (D,), 0.3, 1.5, (), jnp.float32)
    cross_query = normal_values(streams_of[10], (D, D), D ** -0.5, 0.25)
    cross_key = normal_values(streams_of[11], (D, D), D ** -0.5, 0.25)
    cross_value = normal_values(streams_of[12], (D, D), D ** -0.5, 0.25)
    cross_out = normal_values(streams_of[13], (D, D), (D // 16) ** -0.5, 1.0)
    gain_two = jnp.clip(1.0 + 0.15 * jax.random.normal(streams_of[14], (D,), jnp.float32), 0.25, 1.75)
    shift_two = normal_values(streams_of[15], (D,), 0.3, 1.5, (), jnp.float32)
    expand_weight = normal_values(streams_of[16], (D, FF), D ** -0.5, 0.25)
    reduce_weight = normal_values(streams_of[17], (FF, D), (FF // 4) ** -0.5, 0.25)
    gain_three = jnp.clip(1.0 + 0.15 * jax.random.normal(streams_of[18], (D,), jnp.float32), 0.25, 1.75)
    shift_three = normal_values(streams_of[19], (D,), 0.3, 1.5, (), jnp.float32)
    output_cotangent = normal_values(streams_of[20], (ROWS, LEN, D), 1.0, 6.0, ((0, 2), (1, 16)))
    return {"states": states, "memory": memory, "target_segments": target_segments, "memory_segments": memory_segments, "self_query": self_query, "self_key": self_key, "self_value": self_value, "self_out": self_out, "gain_one": gain_one, "shift_one": shift_one, "cross_query": cross_query, "cross_key": cross_key, "cross_value": cross_value, "cross_out": cross_out, "gain_two": gain_two, "shift_two": shift_two, "expand_weight": expand_weight, "reduce_weight": reduce_weight, "gain_three": gain_three, "shift_three": shift_three, "output_cotangent": output_cotangent}


@jax.custom_vjp
def low(v):
    return lax.optimization_barrier(v.astype(jnp.bfloat16)).astype(jnp.float32)

@jax.custom_vjp
def low_back(v):
    return v

def low_keep(v):
    return (low(v), None)

def low_pass(kept, grad):
    return (grad,)

def back_keep(v):
    return (v, None)

def back_low(kept, grad):
    return (low(grad),)
low.defvjp(low_keep, low_pass)
low_back.defvjp(back_keep, back_low)

def product(left, right):
    return jnp.dot(left, right, preferred_element_type=jnp.float32, precision=lax.Precision.HIGHEST)

def layer_norm(hidden, gain, shift):
    center = hidden - lax.optimization_barrier(jnp.mean(hidden, axis=-1, keepdims=True))
    spread = lax.optimization_barrier(jnp.mean(center * center, axis=-1, keepdims=True))
    return center * lax.rsqrt(spread + 1e-05) * gain + shift

def split_heads(values):
    return values.reshape(values.shape[0], HEADS, HEAD_DIM)

def attention(queries, keys, values, query_seg, key_seg, causal):
    length = queries.shape[0]
    block = min(length, 128)
    scale = HEAD_DIM ** (-0.5)
    key_heads = split_heads(keys)
    value_heads = split_heads(values)
    key_pos = jnp.arange(keys.shape[0], dtype=jnp.int32)
    query_pos = jnp.arange(length, dtype=jnp.int32)

    def one_block(parts):
        query_block, seg_block, pos_block = parts
        scores = jnp.einsum('qhd,khd->qhk', query_block, key_heads, precision=lax.Precision.HIGHEST) * scale
        scores = low_back(scores)
        allowed = seg_block[:, None] == key_seg[None, :]
        if causal:
            allowed = allowed & (key_pos[None, :] <= pos_block[:, None])
        allowed = allowed[:, None, :]
        scores = jnp.where(allowed, scores, -1e+30)
        top = lax.optimization_barrier(jnp.max(scores, axis=2, keepdims=True))
        weights = jnp.where(allowed, jnp.exp(scores - top), 0.0)
        probs = weights / lax.optimization_barrier(jnp.sum(weights, axis=2, keepdims=True))
        return jnp.einsum('qhk,khd->qhd', low(probs), value_heads, precision=lax.Precision.HIGHEST)
    blocks = (split_heads(queries).reshape(length // block, block, HEADS, HEAD_DIM), query_seg.reshape(length // block, block), query_pos.reshape(length // block, block))
    return lax.map(jax.checkpoint(one_block), blocks).reshape(length, HEADS * HEAD_DIM)

def decoder_row(states, memory, query_seg, memory_seg, self_query, self_key, self_value, self_out, gain_one, shift_one, cross_query, cross_key, cross_value, cross_out, gain_two, shift_two, expand_weight, reduce_weight, gain_three, shift_three):
    queries = low_back(low(product(states, self_query)))
    keys = low_back(low(product(states, self_key)))
    values = low_back(low(product(states, self_value)))
    attended = low_back(low(attention(queries, keys, values, query_seg, query_seg, True)))
    first = layer_norm(states + low_back(product(attended, self_out)), gain_one, shift_one)
    cross_q = low_back(low(product(low(first), cross_query)))
    memory_keys = low_back(low(product(memory, cross_key)))
    memory_values = low_back(low(product(memory, cross_value)))
    crossed = low_back(low(attention(cross_q, memory_keys, memory_values, query_seg, memory_seg, False)))
    second = layer_norm(first + low_back(product(crossed, cross_out)), gain_two, shift_two)
    gate = low_back(product(low(second), expand_weight))
    hidden = low(jax.nn.silu(gate))
    return layer_norm(second + low_back(product(hidden, reduce_weight)), gain_three, shift_three)

def reference(states, memory, target_segments, memory_segments, self_query, self_key, self_value, self_out, gain_one, shift_one, cross_query, cross_key, cross_value, cross_out, gain_two, shift_two, expand_weight, reduce_weight, gain_three, shift_three, output_cotangent):
    inputs = [states, memory, self_query, self_key, self_value, self_out, gain_one, shift_one, cross_query, cross_key, cross_value, cross_out, gain_two, shift_two, expand_weight, reduce_weight, gain_three, shift_three]
    floats = [item.astype(jnp.float32) for item in inputs]

    def whole(states_f, memory_f, *weights):
        outputs = [decoder_row(states_f[number], memory_f[number], target_segments[number], memory_segments[number], *weights) for number in range(ROWS)]
        return jnp.stack(outputs)
    result, pullback = jax.vjp(whole, *floats)
    grads = pullback(output_cotangent.astype(jnp.float32))
    return (result.astype(jnp.bfloat16), grads[0], grads[1], grads[2], grads[3], grads[4], grads[5], grads[6], grads[7], grads[8], grads[9], grads[10], grads[11], grads[12], grads[13], grads[14], grads[15], grads[16], grads[17])
```

```python
import functools

import jax
import jax.numpy as jnp
from jax import lax
from jax.experimental import pallas as pl
from jax.experimental.pallas import tpu as pltpu
from jax.sharding import PartitionSpec as P

HEADS = 8
HEAD_DIM = 64
MESH = pl.DeviceIdType.MESH
LOW = jnp.bfloat16
EXTENT = {"x": 2, "y": 2, "z": 4}
ORDERS = (("x", "y", "z"), ("y", "x", "z"))


def rows_at(start, size):
    return pl.ds(pl.multiple_of(start, 16), size)


class Place:
    def __init__(self):
        self.row = lax.axis_index("rows")
        self.seq = lax.axis_index("seq")
        self.core = lax.rem(self.seq, 2)
        self.at = {
            "x": self.row,
            "y": lax.rem(self.seq // 2, 2),
            "z": self.seq // 4,
        }

    def sibling(self):
        return (self.row, self.seq + 1 - 2 * self.core)

    def moved(self, dim, step):
        there = lax.rem(self.at[dim] + step, EXTENT[dim])
        if dim == "x":
            return there, (there, self.seq)
        weight = 2 if dim == "y" else 4
        return there, (self.row, self.seq + (there - self.at[dim]) * weight)

    def partners(self):
        found = [self.sibling()]
        for dim, extent in EXTENT.items():
            found += [self.moved(dim, step)[1] for step in range(1, extent)]
        return found


def meet(devices):
    barrier = pltpu.get_barrier_semaphore()
    for device in devices:
        pl.semaphore_signal(barrier, inc=1, device_id=device, device_id_type=MESH)
    pl.semaphore_wait(barrier, len(devices))


class Summed:
    COPIES = 2 * 2 * (1 + 1 + 3) + 1

    def __init__(self, place, part, landing, done, send, recv, start, size, landing_at, first):
        self.place, self.part, self.landing, self.done = place, part, landing, done
        self.send, self.recv = send, recv
        self.start, self.size = start, size
        self.sem = first
        self.plan = []
        half = size // 2
        for color, order in enumerate(ORDERS):
            steps, span = [], half
            base = start + color * half
            for dim in order:
                extent = EXTENT[dim]
                share = span // extent
                own = base + place.at[dim] * share
                steps.append((dim, base, span, share, own, landing_at, self.sem))
                landing_at += share * (extent - 1)
                self.sem += 2 * (extent - 1)
                base, span = own, share
            self.plan.append(steps)
        self.last_sem = self.sem
        self.landing_end = landing_at

    def _out(self, color, step):
        dim, base, span, share, own, at, sem = self.plan[color][step]
        copies = []
        for hop in range(1, EXTENT[dim]):
            there, device = self.place.moved(dim, hop)
            copies.append(
                pltpu.make_async_remote_copy(
                    src_ref=self.part.at[rows_at(base + there * share, share)],
                    dst_ref=self.landing.at[pl.ds(at + (hop - 1) * share, share)],
                    send_sem=self.send.at[sem + hop - 1],
                    recv_sem=self.recv.at[sem + hop - 1],
                    device_id=device,
                    device_id_type=MESH,
                )
            )
        return copies

    def _back(self, color, step):
        dim, base, span, share, own, at, sem = self.plan[color][step]
        extent = EXTENT[dim]
        copies = []
        for hop in range(1, extent):
            there, device = self.place.moved(dim, hop)
            mine = self.done.at[self.place.core, rows_at(own, share)]
            copies.append(
                pltpu.make_async_remote_copy(
                    src_ref=mine,
                    dst_ref=mine,
                    send_sem=self.send.at[sem + extent - 1 + hop - 1],
                    recv_sem=self.recv.at[sem + extent - 1 + hop - 1],
                    device_id=device,
                    device_id_type=MESH,
                )
            )
        return copies

    def _across(self):
        mine = self.done.at[self.place.core, pl.ds(self.start, self.size)]
        return pltpu.make_async_remote_copy(
            src_ref=mine,
            dst_ref=mine,
            send_sem=self.send.at[self.last_sem],
            recv_sem=self.recv.at[self.last_sem],
            device_id=self.place.sibling(),
            device_id_type=MESH,
        )

    def begin(self):
        for color in range(2):
            for copy in self._out(color, 0):
                copy.start()

    def gather(self, step):
        for color in range(2):
            dim, base, span, share, own, at, sem = self.plan[color][step]
            for copy in self._out(color, step):
                copy.wait()
            block = min(share, 128)

            def add(number, carry, color=color, step=step, share=share, own=own, at=at, dim=dim, block=block):
                rows = rows_at(own + number * block, block)
                total = self.part[rows].astype(jnp.float32)
                for hop in range(1, EXTENT[dim]):
                    here = rows_at(at + (hop - 1) * share + number * block, block)
                    total = total + self.landing[here].astype(jnp.float32)
                if step == 2:
                    self.done[self.place.core, rows] = total.astype(LOW)
                else:
                    self.part[rows] = total.astype(LOW)
                return carry

            lax.fori_loop(0, share // block, add, 0)
            for copy in self._out(color, step + 1) if step < 2 else self._back(color, 2):
                copy.start()

    def spread(self, step):
        for color in range(2):
            for copy in self._back(color, step):
                copy.wait()
            if step > 0:
                for copy in self._back(color, step - 1):
                    copy.start()
        if step == 0:
            self._across().start()

    def end(self):
        self._across().wait()


PIECES = (2048, 2048, 2048, 2048)


def sum_kernel(given, small, done_out, small_out, part, landing, done, other, small_in, send, recv):
    place = Place()
    meet(place.partners())
    core = place.core
    copy = pltpu.make_async_remote_copy(
        src_ref=given.at[1 - core],
        dst_ref=other,
        send_sem=send.at[0],
        recv_sem=recv.at[0],
        device_id=place.sibling(),
        device_id_type=MESH,
    )
    copy.start()
    small_out[...] = small[...]
    peers = [("c", 1), ("x", 1), ("y", 1), ("z", 3)]
    slot = 0
    for dim, extent in peers:
        moves = []
        for hop in range(1, extent + 1):
            device = place.sibling() if dim == "c" else place.moved(dim, hop)[1]
            moves.append(
                pltpu.make_async_remote_copy(
                    src_ref=small_out,
                    dst_ref=small_in.at[3 + place.at["z"] if dim == "z" else slot],
                    send_sem=send.at[1 + slot],
                    recv_sem=recv.at[1 + slot],
                    device_id=device,
                    device_id_type=MESH,
                )
            )
            slot += 1
        for move in moves:
            move.start()
        for move in moves:
            move.wait()
        if dim == "z":
            small_in[3 + place.at["z"]] = small_out[...]
            small_out[...] = (small_in[3] + small_in[4]) + (small_in[5] + small_in[6])
        else:
            small_out[...] = small_out[...] + small_in[slot - 1]
    copy.wait()
    pieces, start, landing_at, first = [], 0, 0, 7
    for size in PIECES:
        piece = Summed(place, part, landing, done, send, recv, start, size, landing_at, first)

        def join(number, carry):
            rows = rows_at(start + number * 128, 128)
            part[rows] = (given[core, rows].astype(jnp.float32) + other[rows].astype(jnp.float32)).astype(LOW)
            return carry

        lax.fori_loop(0, size // 128, join, 0)
        piece.begin()
        pieces.append(piece)
        start, landing_at, first = start + size, piece.landing_end, piece.last_sem + 1
    for step in range(3):
        for piece in pieces:
            piece.gather(step)
    for step in (2, 1, 0):
        for piece in pieces:
            piece.spread(step)
    for piece in pieces:
        piece.end()
    done_out[...] = done[...]


def sum_all(large, small):
    rows = sum(PIECES)
    vmem = pl.BlockSpec(memory_space=pltpu.VMEM)
    landing = rows * 15 // 16
    copies = 7 + len(PIECES) * Summed.COPIES
    return pl.pallas_call(
        sum_kernel,
        out_shape=(
            jax.ShapeDtypeStruct((2, rows, 256), LOW),
            jax.ShapeDtypeStruct(small.shape, jnp.float32),
        ),
        in_specs=[vmem, vmem],
        out_specs=(vmem, vmem),
        scratch_shapes=[
            pltpu.VMEM((rows, 256), LOW),
            pltpu.VMEM((landing, 256), LOW),
            pltpu.VMEM((2, rows, 256), LOW),
            pltpu.VMEM((rows, 256), LOW),
            pltpu.VMEM((7,) + small.shape, jnp.float32),
            pltpu.SemaphoreType.DMA((copies,)),
            pltpu.SemaphoreType.DMA((copies,)),
        ],
        compiler_params=pltpu.CompilerParams(
            collective_id=0, has_side_effects=True, vmem_limit_bytes=56 << 20
        ),
    )(large, small)


def halves(grad):
    rows, columns = grad.shape
    blocks = grad.astype(LOW).reshape(rows, 2, columns // 512, 256)
    return blocks.transpose(1, 2, 0, 3).reshape(2, rows * columns // 512, 256)


def whole(block, rows, columns):
    wide = block.reshape(2, columns // 512, rows, 256).transpose(2, 0, 1, 3)
    return wide.reshape(rows, columns).astype(jnp.float32)


def sum_grads(grads):
    large = [grad for grad in grads if grad.ndim == 2]
    small = jnp.stack([grad for grad in grads if grad.ndim == 1] + [jnp.zeros((512,), jnp.float32)] * 2)
    done, small = sum_all(jnp.concatenate([halves(grad) for grad in large], axis=1), small)
    at, number, summed = 0, 0, []
    for grad in grads:
        if grad.ndim == 1:
            summed.append(small[number])
            number += 1
        else:
            size = grad.size // 512
            summed.append(whole(done[:, at : at + size], *grad.shape))
            at += size
    return summed


def layer_norm(hidden, gain, shift):
    center = hidden - jnp.mean(hidden, axis=-1, keepdims=True)
    spread = jnp.mean(center * center, axis=-1, keepdims=True)
    return center * lax.rsqrt(spread + 1e-05) * gain + shift


def split_heads(values):
    return values.reshape(values.shape[0], HEADS, HEAD_DIM)


def forward_dot(left, right):
    return jnp.dot(left, right, preferred_element_type=jnp.float32)


def outer(left, right):
    return lax.dot_general(
        left, right, (((0,), (0,)), ((), ())), preferred_element_type=jnp.float32
    )


def backward_dot(grad, weight):
    return lax.dot_general(
        grad, weight, (((1,), (1,)), ((), ())), preferred_element_type=jnp.float32
    )


def sum_plain(grads):
    return lax.psum(grads, ("rows", "seq"))


def body(
    sum_over_devices,
    states,
    memory,
    target_segments,
    memory_segments,
    self_query,
    self_key,
    self_value,
    self_out,
    gain_one,
    shift_one,
    cross_query,
    cross_key,
    cross_value,
    cross_out,
    gain_two,
    shift_two,
    expand_weight,
    reduce_weight,
    gain_three,
    shift_three,
    output_cotangent,
):
    scale = HEAD_DIM ** (-0.5)
    low_type = jnp.bfloat16
    tokens = states[0]
    local_memory = memory[0]
    query_seg = target_segments[0]
    memory_seg = memory_segments[0]
    count = tokens.shape[0]
    own_start = lax.axis_index("seq") * count
    query_pos = own_start + jnp.arange(count, dtype=jnp.int32)
    queries = forward_dot(tokens, self_query).astype(low_type)
    keys = forward_dot(tokens, self_key).astype(low_type)
    values = forward_dot(tokens, self_value).astype(low_type)
    query_heads = split_heads(queries)
    key_heads = split_heads(keys)
    value_heads = split_heads(values)
    start_state = (
        jnp.full((count, HEADS), -1e30, jnp.float32),
        jnp.zeros((count, HEADS), jnp.float32),
        jnp.zeros((count, HEADS, HEAD_DIM), jnp.float32),
    )
    piece_keys = lax.all_gather(keys, "seq", axis=0, tiled=True)
    piece_values = lax.all_gather(values, "seq", axis=0, tiled=True)
    piece_seg = lax.all_gather(query_seg, "seq", axis=0, tiled=True)
    width = piece_keys.shape[0]
    key_pos = jnp.arange(width, dtype=jnp.int32)
    skip = (
        (jnp.int32(0) > query_pos[-1])
        | (piece_seg[-1] < query_seg[0])
        | (piece_seg[0] > query_seg[-1])
    )

    def compute(state):
        top, total, accum = state
        allowed = (
            (query_seg[:, None] == piece_seg[None, :]) & (key_pos[None, :] <= query_pos[:, None])
        )[:, None, :]
        scores = (
            jnp.einsum(
                "qhd,khd->qhk",
                query_heads,
                split_heads(piece_keys),
                preferred_element_type=jnp.float32,
            )
            * scale
        )
        scores = jnp.where(allowed, scores, -1e30)
        new_top = jnp.maximum(top, jnp.max(scores, axis=2))
        weights = jnp.where(allowed, jnp.exp(scores - new_top[:, :, None]), 0.0)
        total = jnp.sum(weights, axis=2)
        accum = jnp.einsum(
            "qhk,khd->qhd",
            weights.astype(low_type),
            split_heads(piece_values),
            preferred_element_type=jnp.float32,
        )
        return (new_top, total, accum)

    top, total, accum = lax.cond(skip, lambda state: state, compute, start_state)
    attended = accum / total[:, :, None]
    log_total = top + jnp.log(total)
    attended_low = attended.reshape(count, HEADS * HEAD_DIM).astype(low_type)
    first, back_one = jax.vjp(
        layer_norm,
        tokens.astype(jnp.float32) + forward_dot(attended_low, self_out),
        gain_one,
        shift_one,
    )
    first_low = first.astype(low_type)
    cross_q = forward_dot(first_low, cross_query).astype(low_type)
    memory_keys = forward_dot(local_memory, cross_key).astype(low_type)
    memory_values = forward_dot(local_memory, cross_value).astype(low_type)
    all_keys, all_values, all_seg = (
        lax.all_gather(memory_keys, "seq", axis=0, tiled=True),
        lax.all_gather(memory_values, "seq", axis=0, tiled=True),
        lax.all_gather(memory_seg, "seq", axis=0, tiled=True),
    )
    cross_heads = split_heads(cross_q)
    mem_key_heads = split_heads(all_keys)
    mem_value_heads = split_heads(all_values)
    cross_allowed = (query_seg[:, None] == all_seg[None, :])[:, None, :]
    cross_scores = (
        jnp.einsum("qhd,khd->qhk", cross_heads, mem_key_heads, preferred_element_type=jnp.float32)
        * scale
    )
    cross_scores = jnp.where(cross_allowed, cross_scores, -1e30)
    cross_top = jnp.max(cross_scores, axis=2, keepdims=True)
    cross_weights = jnp.where(cross_allowed, jnp.exp(cross_scores - cross_top), 0.0)
    cross_total = jnp.sum(cross_weights, axis=2, keepdims=True)
    cross_probs = cross_weights / cross_total
    cross_probs_low = cross_probs.astype(low_type)
    crossed = jnp.einsum(
        "qhk,khd->qhd", cross_probs_low, mem_value_heads, preferred_element_type=jnp.float32
    )
    crossed_low = crossed.reshape(count, HEADS * HEAD_DIM).astype(low_type)
    second, back_two = jax.vjp(
        layer_norm, first + forward_dot(crossed_low, cross_out), gain_two, shift_two
    )
    second_low = second.astype(low_type)
    gate = forward_dot(second_low, expand_weight)
    hidden, silu_back = jax.vjp(jax.nn.silu, gate)
    hidden_low = hidden.astype(low_type)
    result, back_three = jax.vjp(
        layer_norm, second + forward_dot(hidden_low, reduce_weight), gain_three, shift_three
    )
    layer_output = result.astype(low_type)[None]
    d_third, gain_three_grad, shift_three_grad = back_three(output_cotangent[0].astype(jnp.float32))
    d_branch = d_third.astype(low_type)
    reduce_weight_grad = outer(hidden_low, d_branch)
    d_gate = silu_back(backward_dot(d_branch, reduce_weight))[0].astype(low_type)
    expand_weight_grad = outer(second_low, d_gate)
    d_second = d_third + backward_dot(d_gate, expand_weight)
    d_mid, gain_two_grad, shift_two_grad = back_two(d_second)
    d_cross_branch = d_mid.astype(low_type)
    cross_out_grad = outer(crossed_low, d_cross_branch)
    d_crossed = split_heads(backward_dot(d_cross_branch, cross_out).astype(low_type))
    d_probs = jnp.einsum(
        "qhd,khd->qhk", d_crossed, mem_value_heads, preferred_element_type=jnp.float32
    )
    cross_delta = jnp.sum(cross_probs * d_probs, axis=2, keepdims=True)
    d_scores = (cross_probs * (d_probs - cross_delta)).astype(low_type)
    d_cross_q = (
        (
            jnp.einsum("qhk,khd->qhd", d_scores, mem_key_heads, preferred_element_type=jnp.float32)
            * scale
        )
        .reshape(count, HEADS * HEAD_DIM)
        .astype(low_type)
    )
    key_terms = (
        jnp.einsum("qhk,qhd->khd", d_scores, cross_heads, preferred_element_type=jnp.float32)
        * scale
    ).reshape(-1, HEADS * HEAD_DIM)
    value_terms = jnp.einsum(
        "qhk,qhd->khd", cross_probs_low, d_crossed, preferred_element_type=jnp.float32
    ).reshape(-1, HEADS * HEAD_DIM)
    d_mem_keys, d_mem_values = (
        lax.psum_scatter(key_terms, "seq", scatter_dimension=0, tiled=True),
        lax.psum_scatter(value_terms, "seq", scatter_dimension=0, tiled=True),
    )
    d_mem_keys = d_mem_keys.astype(low_type)
    d_mem_values = d_mem_values.astype(low_type)
    cross_key_grad = outer(local_memory, d_mem_keys)
    cross_value_grad = outer(local_memory, d_mem_values)
    memory_grad = (backward_dot(d_mem_keys, cross_key) + backward_dot(d_mem_values, cross_value))[
        None
    ]
    cross_query_grad = outer(first_low, d_cross_q)
    d_first = d_mid + backward_dot(d_cross_q, cross_query)
    d_start, gain_one_grad, shift_one_grad = back_one(d_first)
    d_self_branch = d_start.astype(low_type)
    self_out_grad = outer(attended_low, d_self_branch)
    d_attended = backward_dot(d_self_branch, self_out).astype(low_type)
    d_heads = split_heads(d_attended)
    delta = jnp.sum(d_heads.astype(jnp.float32) * attended, axis=2)
    all_log, all_delta = (
        lax.all_gather(log_total, "seq", axis=0, tiled=True),
        lax.all_gather(delta, "seq", axis=0, tiled=True),
    )

    def query_part(total_q, piece_keys, piece_values, piece_seg, start):
        key_pos = start + jnp.arange(piece_keys.shape[0], dtype=jnp.int32)
        allowed = (
            (query_seg[:, None] == piece_seg[None, :]) & (key_pos[None, :] <= query_pos[:, None])
        )[:, None, :]
        piece_key_heads = split_heads(piece_keys)
        scores = (
            jnp.einsum(
                "qhd,khd->qhk", query_heads, piece_key_heads, preferred_element_type=jnp.float32
            )
            * scale
        )
        scores = jnp.where(allowed, scores, -1e30)
        probs = jnp.where(allowed, jnp.exp(scores - log_total[:, :, None]), 0.0)
        grads_p = jnp.einsum(
            "qhd,khd->qhk", d_heads, split_heads(piece_values), preferred_element_type=jnp.float32
        )
        grads_s = (probs * (grads_p - delta[:, :, None])).astype(low_type)
        return (
            total_q
            + jnp.einsum(
                "qhk,khd->qhd", grads_s, piece_key_heads, preferred_element_type=jnp.float32
            )
            * scale
        )

    def key_part(
        grad_k, grad_v, piece_queries, piece_grads, piece_seg, piece_log, piece_delta, start
    ):
        piece_pos = start + jnp.arange(piece_queries.shape[0], dtype=jnp.int32)
        allowed = (
            (piece_seg[:, None] == query_seg[None, :]) & (query_pos[None, :] <= piece_pos[:, None])
        )[:, None, :]
        piece_query_heads = split_heads(piece_queries)
        piece_grad_heads = split_heads(piece_grads)
        scores = (
            jnp.einsum(
                "qhd,khd->qhk", piece_query_heads, key_heads, preferred_element_type=jnp.float32
            )
            * scale
        )
        scores = jnp.where(allowed, scores, -1e30)
        probs = jnp.where(allowed, jnp.exp(scores - piece_log[:, :, None]), 0.0)
        grad_v = grad_v + jnp.einsum(
            "qhk,qhd->khd",
            probs.astype(low_type),
            piece_grad_heads,
            preferred_element_type=jnp.float32,
        )
        grads_p = jnp.einsum(
            "qhd,khd->qhk", piece_grad_heads, value_heads, preferred_element_type=jnp.float32
        )
        grads_s = (probs * (grads_p - piece_delta[:, :, None])).astype(low_type)
        grad_k = (
            grad_k
            + jnp.einsum(
                "qhk,qhd->khd", grads_s, piece_query_heads, preferred_element_type=jnp.float32
            )
            * scale
        )
        return (grad_k, grad_v)

    zeros_heads = jnp.zeros((count, HEADS, HEAD_DIM), jnp.float32)
    own_q = query_part(zeros_heads, keys, values, query_seg, own_start)
    own_k, own_v = key_part(
        zeros_heads, zeros_heads, queries, d_attended, query_seg, log_total, delta, own_start
    )

    def both_sides(grads, piece):
        piece_keys, piece_values, piece_queries, piece_grads, piece_seg = piece
        shards = piece_keys.shape[0] // count

        def one_shard(number, state):
            shard_start = number * count

            def rows_of(array):
                return lax.dynamic_slice_in_dim(array, number * count, count, 0)

            shard_seg = rows_of(piece_seg)
            far = (
                (shard_seg[-1] < query_seg[0])
                | (shard_seg[0] > query_seg[-1])
                | (shard_start == own_start)
            )
            branch = jnp.where(far, 0, jnp.where(shard_start < own_start, 1, 2)).astype(jnp.int32)

            def keep_state(inner):
                return inner

            def query_branch(inner):
                return (
                    query_part(
                        inner[0], rows_of(piece_keys), rows_of(piece_values), shard_seg, shard_start
                    ),
                    inner[1],
                    inner[2],
                )

            def key_branch(inner):
                shard_log = lax.dynamic_slice_in_dim(all_log, shard_start, count, 0)
                shard_delta = lax.dynamic_slice_in_dim(all_delta, shard_start, count, 0)
                new_k, new_v = key_part(
                    inner[1],
                    inner[2],
                    rows_of(piece_queries),
                    rows_of(piece_grads),
                    shard_seg,
                    shard_log,
                    shard_delta,
                    shard_start,
                )
                return (inner[0], new_k, new_v)

            return lax.switch(branch, [keep_state, query_branch, key_branch], state)

        return lax.fori_loop(0, shards, one_shard, grads)

    grad_q, grad_k, grad_v = both_sides(
        (own_q, own_k, own_v),
        (
            lax.all_gather(keys, "seq", axis=0, tiled=True),
            lax.all_gather(values, "seq", axis=0, tiled=True),
            lax.all_gather(queries, "seq", axis=0, tiled=True),
            lax.all_gather(d_attended, "seq", axis=0, tiled=True),
            lax.all_gather(query_seg, "seq", axis=0, tiled=True),
        ),
    )
    grad_q = grad_q.reshape(count, HEADS * HEAD_DIM).astype(low_type)
    grad_k = grad_k.reshape(count, HEADS * HEAD_DIM).astype(low_type)
    grad_v = grad_v.reshape(count, HEADS * HEAD_DIM).astype(low_type)
    self_query_grad = outer(tokens, grad_q)
    self_key_grad = outer(tokens, grad_k)
    self_value_grad = outer(tokens, grad_v)
    states_grad = (
        d_start
        + backward_dot(grad_q, self_query)
        + backward_dot(grad_k, self_key)
        + backward_dot(grad_v, self_value)
    )[None]
    summed = sum_over_devices(
        (
            self_query_grad,
            self_key_grad,
            self_value_grad,
            self_out_grad,
            gain_one_grad,
            shift_one_grad,
            cross_query_grad,
            cross_key_grad,
            cross_value_grad,
            cross_out_grad,
            gain_two_grad,
            shift_two_grad,
            expand_weight_grad,
            reduce_weight_grad,
            gain_three_grad,
            shift_three_grad,
        )
    )
    (
        self_query_grad,
        self_key_grad,
        self_value_grad,
        self_out_grad,
        gain_one_grad,
        shift_one_grad,
    ) = summed[0:6]
    (
        cross_query_grad,
        cross_key_grad,
        cross_value_grad,
        cross_out_grad,
        gain_two_grad,
        shift_two_grad,
    ) = summed[6:12]
    expand_weight_grad, reduce_weight_grad, gain_three_grad, shift_three_grad = summed[12:16]
    return (
        layer_output,
        states_grad,
        memory_grad,
        self_query_grad,
        self_key_grad,
        self_value_grad,
        self_out_grad,
        gain_one_grad,
        shift_one_grad,
        cross_query_grad,
        cross_key_grad,
        cross_value_grad,
        cross_out_grad,
        gain_two_grad,
        shift_two_grad,
        expand_weight_grad,
        reduce_weight_grad,
        gain_three_grad,
        shift_three_grad,
    )


def solution(mesh):
    fast = dict(mesh.shape) == {"rows": 2, "seq": 16}
    return jax.shard_map(
        functools.partial(body, sum_grads if fast else sum_plain),
        mesh=mesh,
        in_specs=(
            P("rows", "seq", None),
            P("rows", "seq", None),
            P("rows", "seq"),
            P("rows", "seq"),
            P(),
            P(),
            P(),
            P(),
            P(),
            P(),
            P(),
            P(),
            P(),
            P(),
            P(),
            P(),
            P(),
            P(),
            P(),
            P(),
            P("rows", "seq", None),
        ),
        out_specs=(
            P("rows", "seq", None),
            P("rows", "seq", None),
            P("rows", "seq", None),
            P(),
            P(),
            P(),
            P(),
            P(),
            P(),
            P(),
            P(),
            P(),
            P(),
            P(),
            P(),
            P(),
            P(),
            P(),
            P(),
        ),
        check_vma=False,
    )
```

```python
import inspect
import math
import types

import jax
import jax.numpy as jnp
from jax import lax
from jax.experimental import pallas as pl
from jax.experimental.pallas import tpu as pltpu
from jax.sharding import PartitionSpec as P

HEADS = 8
HEAD_DIM = 64
MESH = pl.DeviceIdType.MESH
LOW = jnp.bfloat16
ROWS, SEQ = "rows", "seq"


def layer_norm(hidden, gain, shift):
    center = hidden - jnp.mean(hidden, axis=-1, keepdims=True)
    spread = jnp.mean(center * center, axis=-1, keepdims=True)
    return center * lax.rsqrt(spread + 1e-05) * gain + shift


def split_heads(values):
    return values.reshape(values.shape[0], HEADS, HEAD_DIM)


def forward_dot(left, right):
    return jnp.dot(left, right, preferred_element_type=jnp.float32)


def outer(left, right):
    return lax.dot_general(
        left, right, (((0,), (0,)), ((), ())), preferred_element_type=jnp.float32
    )


def backward_dot(grad, weight):
    return lax.dot_general(
        grad, weight, (((1,), (1,)), ((), ())), preferred_element_type=jnp.float32
    )


def body(
    states,
    memory,
    target_segments,
    memory_segments,
    self_query,
    self_key,
    self_value,
    self_out,
    gain_one,
    shift_one,
    cross_query,
    cross_key,
    cross_value,
    cross_out,
    gain_two,
    shift_two,
    expand_weight,
    reduce_weight,
    gain_three,
    shift_three,
    output_cotangent,
):
    scale = HEAD_DIM ** (-0.5)
    low_type = jnp.bfloat16
    tokens = states[0]
    local_memory = memory[0]
    query_seg = target_segments[0]
    memory_seg = memory_segments[0]
    count = tokens.shape[0]
    own_start = lax.axis_index(SEQ) * count
    query_pos = own_start + jnp.arange(count, dtype=jnp.int32)
    queries = forward_dot(tokens, self_query).astype(low_type)
    keys = forward_dot(tokens, self_key).astype(low_type)
    values = forward_dot(tokens, self_value).astype(low_type)
    query_heads = split_heads(queries)
    key_heads = split_heads(keys)
    value_heads = split_heads(values)
    start_state = (
        jnp.full((count, HEADS), -1e30, jnp.float32),
        jnp.zeros((count, HEADS), jnp.float32),
        jnp.zeros((count, HEADS, HEAD_DIM), jnp.float32),
    )
    piece_keys = lax.all_gather(keys, SEQ, axis=0, tiled=True)
    piece_values = lax.all_gather(values, SEQ, axis=0, tiled=True)
    piece_seg = lax.all_gather(query_seg, SEQ, axis=0, tiled=True)
    width = piece_keys.shape[0]
    key_pos = jnp.arange(width, dtype=jnp.int32)
    skip = (
        (jnp.int32(0) > query_pos[-1])
        | (piece_seg[-1] < query_seg[0])
        | (piece_seg[0] > query_seg[-1])
    )

    def compute(state):
        top, total, accum = state
        allowed = (
            (query_seg[:, None] == piece_seg[None, :]) & (key_pos[None, :] <= query_pos[:, None])
        )[:, None, :]
        scores = (
            jnp.einsum(
                "qhd,khd->qhk",
                query_heads,
                split_heads(piece_keys),
                preferred_element_type=jnp.float32,
            )
            * scale
        )
        scores = jnp.where(allowed, scores, -1e30)
        new_top = jnp.maximum(top, jnp.max(scores, axis=2))
        weights = jnp.where(allowed, jnp.exp(scores - new_top[:, :, None]), 0.0)
        total = jnp.sum(weights, axis=2)
        accum = jnp.einsum(
            "qhk,khd->qhd",
            weights.astype(low_type),
            split_heads(piece_values),
            preferred_element_type=jnp.float32,
        )
        return (new_top, total, accum)

    top, total, accum = lax.cond(skip, lambda state: state, compute, start_state)
    attended = accum / total[:, :, None]
    log_total = top + jnp.log(total)
    attended_low = attended.reshape(count, HEADS * HEAD_DIM).astype(low_type)
    first, back_one = jax.vjp(
        layer_norm,
        tokens.astype(jnp.float32) + forward_dot(attended_low, self_out),
        gain_one,
        shift_one,
    )
    first_low = first.astype(low_type)
    cross_q = forward_dot(first_low, cross_query).astype(low_type)
    memory_keys = forward_dot(local_memory, cross_key).astype(low_type)
    memory_values = forward_dot(local_memory, cross_value).astype(low_type)
    all_keys, all_values, all_seg = (
        lax.all_gather(memory_keys, SEQ, axis=0, tiled=True),
        lax.all_gather(memory_values, SEQ, axis=0, tiled=True),
        lax.all_gather(memory_seg, SEQ, axis=0, tiled=True),
    )
    cross_heads = split_heads(cross_q)
    mem_key_heads = split_heads(all_keys)
    mem_value_heads = split_heads(all_values)
    cross_allowed = (query_seg[:, None] == all_seg[None, :])[:, None, :]
    cross_scores = (
        jnp.einsum("qhd,khd->qhk", cross_heads, mem_key_heads, preferred_element_type=jnp.float32)
        * scale
    )
    cross_scores = jnp.where(cross_allowed, cross_scores, -1e30)
    cross_top = jnp.max(cross_scores, axis=2, keepdims=True)
    cross_weights = jnp.where(cross_allowed, jnp.exp(cross_scores - cross_top), 0.0)
    cross_total = jnp.sum(cross_weights, axis=2, keepdims=True)
    cross_probs = cross_weights / cross_total
    cross_probs_low = cross_probs.astype(low_type)
    crossed = jnp.einsum(
        "qhk,khd->qhd", cross_probs_low, mem_value_heads, preferred_element_type=jnp.float32
    )
    crossed_low = crossed.reshape(count, HEADS * HEAD_DIM).astype(low_type)
    second, back_two = jax.vjp(
        layer_norm, first + forward_dot(crossed_low, cross_out), gain_two, shift_two
    )
    second_low = second.astype(low_type)
    gate = forward_dot(second_low, expand_weight)
    hidden, silu_back = jax.vjp(jax.nn.silu, gate)
    hidden_low = hidden.astype(low_type)
    result, back_three = jax.vjp(
        layer_norm, second + forward_dot(hidden_low, reduce_weight), gain_three, shift_three
    )
    layer_output = result.astype(low_type)[None]
    d_third, gain_three_grad, shift_three_grad = back_three(output_cotangent[0].astype(jnp.float32))
    d_branch = d_third.astype(low_type)
    reduce_weight_grad = outer(hidden_low, d_branch)
    d_gate = silu_back(backward_dot(d_branch, reduce_weight))[0].astype(low_type)
    expand_weight_grad = outer(second_low, d_gate)
    d_second = d_third + backward_dot(d_gate, expand_weight)
    d_mid, gain_two_grad, shift_two_grad = back_two(d_second)
    d_cross_branch = d_mid.astype(low_type)
    cross_out_grad = outer(crossed_low, d_cross_branch)
    d_crossed = split_heads(backward_dot(d_cross_branch, cross_out).astype(low_type))
    d_probs = jnp.einsum(
        "qhd,khd->qhk", d_crossed, mem_value_heads, preferred_element_type=jnp.float32
    )
    cross_delta = jnp.sum(cross_probs * d_probs, axis=2, keepdims=True)
    d_scores = (cross_probs * (d_probs - cross_delta)).astype(low_type)
    d_cross_q = (
        (
            jnp.einsum("qhk,khd->qhd", d_scores, mem_key_heads, preferred_element_type=jnp.float32)
            * scale
        )
        .reshape(count, HEADS * HEAD_DIM)
        .astype(low_type)
    )
    key_terms = (
        jnp.einsum("qhk,qhd->khd", d_scores, cross_heads, preferred_element_type=jnp.float32)
        * scale
    ).reshape(-1, HEADS * HEAD_DIM)
    value_terms = jnp.einsum(
        "qhk,qhd->khd", cross_probs_low, d_crossed, preferred_element_type=jnp.float32
    ).reshape(-1, HEADS * HEAD_DIM)
    d_mem_keys, d_mem_values = (
        lax.psum_scatter(key_terms, SEQ, scatter_dimension=0, tiled=True),
        lax.psum_scatter(value_terms, SEQ, scatter_dimension=0, tiled=True),
    )
    d_mem_keys = d_mem_keys.astype(low_type)
    d_mem_values = d_mem_values.astype(low_type)
    cross_key_grad = outer(local_memory, d_mem_keys)
    cross_value_grad = outer(local_memory, d_mem_values)
    memory_grad = (backward_dot(d_mem_keys, cross_key) + backward_dot(d_mem_values, cross_value))[
        None
    ]
    cross_query_grad = outer(first_low, d_cross_q)
    d_first = d_mid + backward_dot(d_cross_q, cross_query)
    d_start, gain_one_grad, shift_one_grad = back_one(d_first)
    d_self_branch = d_start.astype(low_type)
    self_out_grad = outer(attended_low, d_self_branch)
    d_attended = backward_dot(d_self_branch, self_out).astype(low_type)
    d_heads = split_heads(d_attended)
    delta = jnp.sum(d_heads.astype(jnp.float32) * attended, axis=2)
    all_log, all_delta = (
        lax.all_gather(log_total, SEQ, axis=0, tiled=True),
        lax.all_gather(delta, SEQ, axis=0, tiled=True),
    )

    def query_part(total_q, piece_keys, piece_values, piece_seg, start):
        key_pos = start + jnp.arange(piece_keys.shape[0], dtype=jnp.int32)
        allowed = (
            (query_seg[:, None] == piece_seg[None, :]) & (key_pos[None, :] <= query_pos[:, None])
        )[:, None, :]
        piece_key_heads = split_heads(piece_keys)
        scores = (
            jnp.einsum(
                "qhd,khd->qhk", query_heads, piece_key_heads, preferred_element_type=jnp.float32
            )
            * scale
        )
        scores = jnp.where(allowed, scores, -1e30)
        probs = jnp.where(allowed, jnp.exp(scores - log_total[:, :, None]), 0.0)
        grads_p = jnp.einsum(
            "qhd,khd->qhk", d_heads, split_heads(piece_values), preferred_element_type=jnp.float32
        )
        grads_s = (probs * (grads_p - delta[:, :, None])).astype(low_type)
        return (
            total_q
            + jnp.einsum(
                "qhk,khd->qhd", grads_s, piece_key_heads, preferred_element_type=jnp.float32
            )
            * scale
        )

    def key_part(
        grad_k, grad_v, piece_queries, piece_grads, piece_seg, piece_log, piece_delta, start
    ):
        piece_pos = start + jnp.arange(piece_queries.shape[0], dtype=jnp.int32)
        allowed = (
            (piece_seg[:, None] == query_seg[None, :]) & (query_pos[None, :] <= piece_pos[:, None])
        )[:, None, :]
        piece_query_heads = split_heads(piece_queries)
        piece_grad_heads = split_heads(piece_grads)
        scores = (
            jnp.einsum(
                "qhd,khd->qhk", piece_query_heads, key_heads, preferred_element_type=jnp.float32
            )
            * scale
        )
        scores = jnp.where(allowed, scores, -1e30)
        probs = jnp.where(allowed, jnp.exp(scores - piece_log[:, :, None]), 0.0)
        grad_v = grad_v + jnp.einsum(
            "qhk,qhd->khd",
            probs.astype(low_type),
            piece_grad_heads,
            preferred_element_type=jnp.float32,
        )
        grads_p = jnp.einsum(
            "qhd,khd->qhk", piece_grad_heads, value_heads, preferred_element_type=jnp.float32
        )
        grads_s = (probs * (grads_p - piece_delta[:, :, None])).astype(low_type)
        grad_k = (
            grad_k
            + jnp.einsum(
                "qhk,qhd->khd", grads_s, piece_query_heads, preferred_element_type=jnp.float32
            )
            * scale
        )
        return (grad_k, grad_v)

    zeros_heads = jnp.zeros((count, HEADS, HEAD_DIM), jnp.float32)
    own_q = query_part(zeros_heads, keys, values, query_seg, own_start)
    own_k, own_v = key_part(
        zeros_heads, zeros_heads, queries, d_attended, query_seg, log_total, delta, own_start
    )

    def both_sides(grads, piece):
        piece_keys, piece_values, piece_queries, piece_grads, piece_seg = piece
        shards = piece_keys.shape[0] // count

        def one_shard(number, state):
            shard_start = number * count

            def rows_of(array):
                return lax.dynamic_slice_in_dim(array, number * count, count, 0)

            shard_seg = rows_of(piece_seg)
            far = (
                (shard_seg[-1] < query_seg[0])
                | (shard_seg[0] > query_seg[-1])
                | (shard_start == own_start)
            )
            branch = jnp.where(far, 0, jnp.where(shard_start < own_start, 1, 2)).astype(jnp.int32)

            def keep_state(inner):
                return inner

            def query_branch(inner):
                return (
                    query_part(
                        inner[0], rows_of(piece_keys), rows_of(piece_values), shard_seg, shard_start
                    ),
                    inner[1],
                    inner[2],
                )

            def key_branch(inner):
                shard_log = lax.dynamic_slice_in_dim(all_log, shard_start, count, 0)
                shard_delta = lax.dynamic_slice_in_dim(all_delta, shard_start, count, 0)
                new_k, new_v = key_part(
                    inner[1],
                    inner[2],
                    rows_of(piece_queries),
                    rows_of(piece_grads),
                    shard_seg,
                    shard_log,
                    shard_delta,
                    shard_start,
                )
                return (inner[0], new_k, new_v)

            return lax.switch(branch, [keep_state, query_branch, key_branch], state)

        return lax.fori_loop(0, shards, one_shard, grads)

    grad_q, grad_k, grad_v = both_sides(
        (own_q, own_k, own_v),
        (
            lax.all_gather(keys, SEQ, axis=0, tiled=True),
            lax.all_gather(values, SEQ, axis=0, tiled=True),
            lax.all_gather(queries, SEQ, axis=0, tiled=True),
            lax.all_gather(d_attended, SEQ, axis=0, tiled=True),
            lax.all_gather(query_seg, SEQ, axis=0, tiled=True),
        ),
    )
    grad_q = grad_q.reshape(count, HEADS * HEAD_DIM).astype(low_type)
    grad_k = grad_k.reshape(count, HEADS * HEAD_DIM).astype(low_type)
    grad_v = grad_v.reshape(count, HEADS * HEAD_DIM).astype(low_type)
    self_query_grad = outer(tokens, grad_q)
    self_key_grad = outer(tokens, grad_k)
    self_value_grad = outer(tokens, grad_v)
    states_grad = (
        d_start
        + backward_dot(grad_q, self_query)
        + backward_dot(grad_k, self_key)
        + backward_dot(grad_v, self_value)
    )[None]
    summed = lax.psum(
        (
            self_query_grad,
            self_key_grad,
            self_value_grad,
            self_out_grad,
            gain_one_grad,
            shift_one_grad,
            cross_query_grad,
            cross_key_grad,
            cross_value_grad,
            cross_out_grad,
            gain_two_grad,
            shift_two_grad,
            expand_weight_grad,
            reduce_weight_grad,
            gain_three_grad,
            shift_three_grad,
        ),
        (ROWS, SEQ),
    )
    (
        self_query_grad,
        self_key_grad,
        self_value_grad,
        self_out_grad,
        gain_one_grad,
        shift_one_grad,
    ) = summed[0:6]
    (
        cross_query_grad,
        cross_key_grad,
        cross_value_grad,
        cross_out_grad,
        gain_two_grad,
        shift_two_grad,
    ) = summed[6:12]
    expand_weight_grad, reduce_weight_grad, gain_three_grad, shift_three_grad = summed[12:16]
    return (
        layer_output,
        states_grad,
        memory_grad,
        self_query_grad,
        self_key_grad,
        self_value_grad,
        self_out_grad,
        gain_one_grad,
        shift_one_grad,
        cross_query_grad,
        cross_key_grad,
        cross_value_grad,
        cross_out_grad,
        gain_two_grad,
        shift_two_grad,
        expand_weight_grad,
        reduce_weight_grad,
        gain_three_grad,
        shift_three_grad,
    )


EXTENT = {"x": 2, "y": 2, "z": 4}
ORDERS = (("x", "y", "z"), ("y", "x", "z"))
CHIPS = 8
TOKENS = 128
MODEL = 512
HIDDEN = 2048
SLOTS = 8
AT = types.SimpleNamespace(
    reduce=0,
    expand=2048,
    cross_out=4096,
    memory=4608,
    cross_query=5120,
    self_out=5632,
    self_query=6144,
    self_key=6656,
    self_value=7168,
    cross_key=7680,
    cross_value=8192,
)
SUMMED_ROWS = 7680
DONE_ROWS = 8704
PIECES = (1024, 1024, 1024, 1024, 1024, 1024, 1536)
SEMAPHORES = 320


def rows_at(start, size):
    return pl.ds(pl.multiple_of(start, 16), size)


def dot(left, right):
    return jnp.dot(left, right, preferred_element_type=jnp.float32)


def dot_rows(left, right):
    return lax.dot_general(left, right, (((1,), (1,)), ((), ())), preferred_element_type=jnp.float32)


def dot_tokens(left, right):
    return lax.dot_general(left, right, (((0,), (0,)), ((), ())), preferred_element_type=jnp.float32)


def left_lanes(rows):
    return lax.broadcasted_iota(jnp.int32, (rows, 128), 1) < 64


def turned(block):
    return pltpu.roll(block, 64, 1)


def fold_pair(block):
    top, bottom, left = block[:64], block[64:], left_lanes(64)
    return jnp.where(left, top, turned(bottom)), jnp.where(left, turned(top), bottom)


def unfold_pair(even, odd):
    left = left_lanes(64)
    top = jnp.where(left, even, turned(odd))
    bottom = jnp.where(left, turned(even), odd)
    return jnp.concatenate([top, bottom], axis=0)


class Place:
    def __init__(self):
        self.row = lax.axis_index(ROWS)
        self.seq = lax.axis_index(SEQ)
        self.core = lax.rem(self.seq, 2)
        self.chip = self.seq // 2
        self.at = {
            "x": self.row,
            "y": lax.rem(self.chip, 2),
            "z": self.seq // 4,
        }

    def sibling(self):
        return (self.row, self.seq + 1 - 2 * self.core)

    def on_chip(self, chip):
        return (self.row, 2 * chip + self.core)

    def moved(self, dim, step):
        there = lax.rem(self.at[dim] + step, EXTENT[dim])
        if dim == "x":
            return there, (there, self.seq)
        weight = 2 if dim == "y" else 4
        return there, (self.row, self.seq + (there - self.at[dim]) * weight)


class Links:
    def __init__(self, place, send, recv):
        self.place, self.send, self.recv = place, send, recv
        self.used = 0

    def take(self, count):
        first = self.used
        self.used += count
        assert self.used <= SEMAPHORES
        return first

    def copy(self, src, dst, device, sent, arrived):
        return pltpu.make_async_remote_copy(
            src_ref=src,
            dst_ref=dst,
            send_sem=self.send.at[sent],
            recv_sem=self.recv.at[arrived],
            device_id=device,
            device_id_type=MESH,
        )

    def local(self, src, dst, arrived):
        return pltpu.make_async_copy(src, dst, self.recv.at[arrived])


class Spread:
    def __init__(self, links, out, into):
        self.links, self.out, self.into = links, out, into
        self.base = links.take(CHIPS)
        self.chip = links.place.chip

    def _copy(self, there, sent):
        return self.links.copy(
            self.out.at[there],
            self.into.at[self.chip],
            self.links.place.on_chip(there),
            self.base + sent,
            self.base + self.chip,
        )

    def _own(self):
        return self.links.local(self.out.at[self.chip], self.into.at[self.chip], self.base + self.chip)

    def start_all(self):
        for hop in range(1, CHIPS):
            self._copy(lax.rem(self.chip + hop, CHIPS), hop).start()
        self._own().start()

    def end_all(self):
        for hop in range(1, CHIPS):
            self._copy(lax.rem(self.chip + hop, CHIPS), hop).wait_send()

    def start(self, there):
        @pl.when(self.chip != there)
        def _():
            self._copy(there, there).start()

        @pl.when(self.chip == there)
        def _():
            self._own().start()

    def end(self, there):
        @pl.when(self.chip != there)
        def _():
            self._copy(there, there).wait_send()

    def wait_from(self, chip):
        self.links.local(self.into.at[chip], self.into.at[chip], self.base + chip).wait()


class Pair:
    def __init__(self, links, src, dst):
        self.made = None
        self.links, self.src, self.dst = links, src, dst
        self.sem = links.take(1)

    def _copy(self):
        return self.links.copy(self.src, self.dst, self.links.place.sibling(), self.sem, self.sem)

    def start(self):
        self._copy().start()

    def wait(self):
        self._copy().wait()


class Summed:
    def __init__(self, links, part, landing, done, start, size, landing_at):
        self.links, self.place = links, links.place
        self.part, self.landing, self.done = part, landing, done
        self.start, self.size = start, size
        self.plan = []
        half = size // 2
        for color, order in enumerate(ORDERS):
            steps, span = [], half
            base = start + color * half
            for dim in order:
                extent = EXTENT[dim]
                share = span // extent
                own = base + self.place.at[dim] * share
                sem = links.take(2 * (extent - 1))
                steps.append((dim, base, share, own, landing_at, sem))
                landing_at += share * (extent - 1)
                base, span = own, share
            self.plan.append(steps)
        self.landing_end = landing_at
        mine = done.at[self.place.core, pl.ds(start, size)]
        self.across = Pair(links, mine, mine)

    def _out(self, color, step):
        dim, base, share, own, at, sem = self.plan[color][step]
        copies = []
        for hop in range(1, EXTENT[dim]):
            there, device = self.place.moved(dim, hop)
            src = self.part.at[rows_at(base + there * share, share)]
            dst = self.landing.at[pl.ds(at + (hop - 1) * share, share)]
            copies.append(self.links.copy(src, dst, device, sem + hop - 1, sem + hop - 1))
        return copies

    def _back(self, color, step):
        dim, base, share, own, at, sem = self.plan[color][step]
        sem = sem + EXTENT[dim] - 1
        mine = self.done.at[self.place.core, rows_at(own, share)]
        copies = []
        for hop in range(1, EXTENT[dim]):
            device = self.place.moved(dim, hop)[1]
            copies.append(self.links.copy(mine, mine, device, sem + hop - 1, sem + hop - 1))
        return copies

    def begin(self):
        for color in range(2):
            for copy in self._out(color, 0):
                copy.start()

    def gather(self, step):
        for color in range(2):
            dim, base, share, own, at, sem = self.plan[color][step]
            for copy in self._out(color, step):
                copy.wait()
            block = math.gcd(share, 128)

            def add(number, carry, step=step, share=share, own=own, at=at, dim=dim, block=block):
                rows = rows_at(own + number * block, block)
                total = self.part[rows].astype(jnp.float32)
                for hop in range(1, EXTENT[dim]):
                    here = rows_at(at + (hop - 1) * share + number * block, block)
                    total = total + self.landing[here].astype(jnp.float32)
                if step == 2:
                    self.done[self.place.core, rows] = total.astype(LOW)
                else:
                    self.part[rows] = total.astype(LOW)
                return carry

            lax.fori_loop(0, share // block, add, 0)
            for copy in self._out(color, step + 1) if step < 2 else self._back(color, 2):
                copy.start()

    def spread(self, step):
        for color in range(2):
            for copy in self._back(color, step):
                copy.wait()
            if step > 0:
                for copy in self._back(color, step - 1):
                    copy.start()
        if step == 0:
            self.across.start()

    def advance(self, event):
        if event < 3:
            self.gather(event)
        elif event < 6:
            self.spread(5 - event)
        else:
            self.across.wait()


class Rows:
    def __init__(self, links, held, landing):
        self.links, self.place = links, links.place
        self.held, self.landing = held, landing
        self.base = links.take(6)

    def _copies(self, step):
        if step < 3:
            device = self.place.sibling() if step == 0 else self.place.moved("xy"[step - 1], 1)[1]
            return [self.links.copy(self.held, self.landing.at[step], device, self.base + step, self.base + step)]
        here = self.landing.at[3 + self.place.at["z"]]
        sem = self.base + 2
        return [
            self.links.copy(self.held, here, self.place.moved("z", hop)[1], sem + hop, sem + hop)
            for hop in (1, 2, 3)
        ]

    def begin(self):
        for copy in self._copies(0):
            copy.start()

    def advance(self, event):
        for copy in self._copies(event):
            copy.wait()
        if event < 3:
            self.held[...] = self.held[...] + self.landing[event]
            for copy in self._copies(event + 1):
                copy.start()
        else:
            self.landing[3 + self.place.at["z"]] = self.held[...]
            lower, upper = self.landing[3] + self.landing[4], self.landing[5] + self.landing[6]
            self.held[...] = lower + upper


def normed(hidden, gain, shift):
    center = hidden - jnp.mean(hidden, axis=-1, keepdims=True)
    scale = lax.rsqrt(jnp.mean(center * center, axis=-1, keepdims=True) + 1e-05)
    unit = center * scale
    return unit * gain + shift, unit, scale


def normed_back(grad, unit, scale, gain):
    d_unit = grad * gain
    mean = jnp.mean(d_unit, axis=-1, keepdims=True)
    slope = jnp.mean(d_unit * unit, axis=-1, keepdims=True)
    d_hidden = scale * (d_unit - mean - unit * slope)
    return d_hidden, jnp.sum(grad * unit, axis=0, keepdims=True), jnp.sum(grad, axis=0, keepdims=True)


WEIGHTS = dict(
    self_query=(MODEL, MODEL),
    self_key=(MODEL, MODEL),
    self_value=(MODEL, MODEL),
    self_out=(MODEL, MODEL),
    cross_query=(MODEL, MODEL),
    cross_key=(MODEL, MODEL),
    cross_value=(MODEL, MODEL),
    cross_out=(MODEL, MODEL),
    expand_weight=(MODEL, HIDDEN),
    reduce_weight=(HIDDEN, MODEL),
)
LEFT = dict(states=512, attended=512, first=512, crossed=512, second=512, hidden=2048)
RIGHT = dict(d_branch=512, d_gate=2048, d_cross=512, d_cross_q=512, d_self=512, d_q=512, d_k=512, d_v=512)


def scratch_of():
    f32 = jnp.float32
    shapes = dict(
        q_out=((CHIPS, 64, 128), LOW),
        q_in=((CHIPS, 64, 128), LOW),
        q_pad=((CHIPS, 128, 128), LOW),
        kv_out=((CHIPS, 144, 128), LOW),
        kv_in=((2 * CHIPS, 144, 128), LOW),
        mem_out=((16, 256), LOW),
        mem_in=((2, CHIPS, 16, 256), LOW),
        mem_f32=((TOKENS, MODEL), f32),
        mem_rows=((2, TOKENS, MODEL), LOW),
        mem_k=((TOKENS, MODEL), LOW),
        mem_v=((TOKENS, MODEL), LOW),
        ids=((16, 128), f32),
        probs=((CHIPS, 128, 2048), LOW),
        accum=((CHIPS, 128, 128), f32),
        a_out=((CHIPS, 64, 128), LOW),
        a_in=((CHIPS, 64, 128), LOW),
        da_out=((CHIPS, 64, 128), LOW),
        da_in=((CHIPS, 64, 128), LOW),
        dq_out=((CHIPS, 64, 128), LOW),
        dq_in=((CHIPS, 64, 128), LOW),
        dkv_out=((CHIPS, 128, 128), LOW),
        dkv_in=((CHIPS, 128, 128), LOW),
        dkv=((2 * CHIPS, 128, 128), f32),
        dkv_pair=((CHIPS, 128, 128), f32),
        gate=((TOKENS, HIDDEN), f32),
        cross_p=((8 * TOKENS, 128), f32),
        cross_q=((TOKENS, MODEL), LOW),
        crossed_d=((TOKENS, MODEL), LOW),
        d_mem=((2, TOKENS, MODEL), f32),
        d_mem_out=((2, TOKENS, 256), LOW),
        d_mem_pair=((2, TOKENS, 256), LOW),
        part=((SUMMED_ROWS, 256), LOW),
        landing=((SUMMED_ROWS * 15 // 16, 256), LOW),
        done=((2, DONE_ROWS, 256), LOW),
        rows_held=((SLOTS, MODEL), f32),
        rows_in=((7, SLOTS, MODEL), f32),
        d_start=((TOKENS, MODEL), f32),
    )
    for name, width in LEFT.items():
        shapes["left_" + name] = ((2 * TOKENS, width), LOW)
    for name, width in RIGHT.items():
        shapes["full_" + name] = ((TOKENS, width), LOW)
        shapes["right_" + name] = ((2 * TOKENS, width // 2), LOW)
    for name, shape in WEIGHTS.items():
        shapes["w_" + name] = (shape, LOW)
    return shapes


VECTORS = tuple(name for name in inspect.signature(body).parameters if name[:4] in ("gain", "shif"))
GIVEN = ("states", "memory", "target_segments", "memory_segments", "output_cotangent") + VECTORS
MADE = ("layer_output", "states_grad", "memory_grad", "rows", "sums")


def layer_kernel(*refs):
    names = GIVEN + tuple(WEIGHTS) + MADE + tuple(scratch_of()) + ("send", "recv", "fetch")
    assert len(names) == len(refs)
    r = types.SimpleNamespace(**dict(zip(names, refs)))
    place = Place()
    links = Links(place, r.send, r.recv)
    row, seq, core, chip = place.row, place.seq, place.core, place.chip
    scale = HEAD_DIM**-0.5
    f32 = jnp.float32

    fetches = {}
    for number, name in enumerate(WEIGHTS):
        fetches[name] = pltpu.make_async_copy(getattr(r, name), getattr(r, "w_" + name), r.fetch.at[number])
        fetches[name].start()

    def weight(name):
        if fetches.get(name) is not None:
            fetches[name].wait()
            fetches[name] = None
        return getattr(r, "w_" + name)

    barrier = pltpu.get_barrier_semaphore()
    friends = [place.sibling(), place.moved("x", 1)[1]]
    friends += [place.on_chip(lax.rem(chip + hop, CHIPS)) for hop in range(1, CHIPS)]
    for friend in friends:
        pl.semaphore_signal(barrier, inc=1, device_id=friend, device_id_type=MESH)

    own_rows = pl.ds(pl.multiple_of(core * TOKENS, TOKENS), TOKENS)
    lefts, rights = {}, {}

    def give_left(name):
        ref = getattr(r, "left_" + name).at[own_rows]
        lefts[name] = Pair(links, ref, ref)
        lefts[name].start()

    def left(name):
        if lefts[name] is not None:
            lefts[name].wait()
            lefts[name] = None
        return getattr(r, "left_" + name)

    def give_right(name):
        full, both = getattr(r, "full_" + name), getattr(r, "right_" + name)
        half = RIGHT[name] // 2
        other = full.at[:, pl.ds(pl.multiple_of((1 - core) * half, half), half)]
        both[own_rows, :] = full[:, pl.ds(pl.multiple_of(core * half, half), half)]
        rights[name] = Pair(links, other, both.at[own_rows])
        rights[name].start()

    def right(name):
        if rights[name] is not None:
            rights[name].wait()
            rights[name] = None
        return getattr(r, "right_" + name)

    tokens = r.states[...]
    r.left_states[own_rows, :] = tokens
    queries = dot(tokens, weight("self_query")[...]) * scale
    keys = dot(tokens, weight("self_key")[...])
    values = dot(tokens, weight("self_value")[...])
    r.ids[...] = jnp.zeros((16, 128), f32)
    r.ids[0:1, :] = r.target_segments[...].astype(f32)
    r.ids[1:2, 0:8] = r.memory_segments[...].astype(f32)
    ids = r.ids[...].astype(LOW)
    left128 = left_lanes(128)
    for pair in range(4):
        lanes = slice(128 * pair, 128 * pair + 128)
        even, odd = fold_pair(queries[:, lanes])
        r.q_out[2 * pair] = even.astype(LOW)
        r.q_out[2 * pair + 1] = odd.astype(LOW)
        key_pair, value_pair = keys[:, lanes], values[:, lanes]
        r.kv_out[2 * pair, 0:128] = jnp.where(left128, key_pair, turned(value_pair)).astype(LOW)
        r.kv_out[2 * pair + 1, 0:128] = jnp.where(left128, turned(key_pair), value_pair).astype(LOW)
        r.kv_out[2 * pair, 128:144] = ids
        r.kv_out[2 * pair + 1, 128:144] = ids
    memory = r.memory[...].astype(f32)
    r.mem_out[...] = jnp.concatenate([memory[:, :256], memory[:, 256:]], axis=0).astype(LOW)

    pl.semaphore_wait(barrier, len(friends))
    kv_base = links.take(CHIPS)
    kv_send = links.take(CHIPS)

    def kv_copy(hop):
        there = lax.rem(chip + hop, CHIPS)
        return links.copy(r.kv_out.at[there], r.kv_in.at[seq], place.on_chip(there), kv_send + hop, kv_base + chip)

    def kv_own():
        return links.local(r.kv_out.at[chip], r.kv_in.at[seq], kv_base + chip)

    kv_own().start()
    for hop in range(1, CHIPS):
        kv_copy(hop).start()
    q_spread = Spread(links, r.q_out, r.q_in)
    q_spread.start_all()
    mem_base = links.take(CHIPS)
    mem_send = links.take(CHIPS)

    def mem_copy(hop):
        there = lax.rem(chip + hop, CHIPS)
        return links.copy(r.mem_out, r.mem_in.at[core, chip], place.on_chip(there), mem_send + hop, mem_base + chip)

    def mem_own():
        return links.local(r.mem_out, r.mem_in.at[core, chip], mem_base + chip)

    mem_own().start()
    for hop in range(1, CHIPS):
        mem_copy(hop).start()
    give_left("states")

    kv_on = [Pair(links, r.kv_in.at[2 * source + core], r.kv_in.at[2 * source + core]) for source in range(CHIPS)]

    def kv_pass(source):
        slot = r.kv_in.at[2 * source + core]
        links.local(slot, slot, kv_base + source).wait()
        kv_on[source].start()

    def count(slot, line, number):
        found = r.kv_in[slot, 128:144].astype(f32)[line : line + 1]
        return jnp.sum(jnp.where(found == number, 1.0, 0.0), axis=1, keepdims=True)

    def first_seen(position, first_one, first_two):
        if first_two is None:
            return jnp.where(position < first_one, 0.0, first_one)
        return jnp.where(position < first_one, 0.0, jnp.where(position < first_two, first_one, first_two))

    kv_pass(0)
    a_spread = Spread(links, r.a_out, r.a_in)
    length = 2 * CHIPS * TOKENS
    for source in range(CHIPS):
        if source + 1 < CHIPS:
            kv_pass(source + 1)
        q_spread.wait_from(source)
        kv_on[source].wait()
        width = 256 * (source + 1)
        folded = r.q_in[source].astype(f32)
        left64 = left_lanes(64)
        padded = jnp.concatenate([jnp.where(left64, folded, 0.0), jnp.where(left64, turned(folded), 0.0)], axis=0)
        padded = padded.astype(LOW)
        r.q_pad[source] = padded
        both = r.kv_in[0 : 2 * source + 2, 0:128].reshape(width, 128)
        scores = dot_rows(padded, both)
        place_q = (core * TOKENS + 2 * source * TOKENS + lax.broadcasted_iota(jnp.int32, (128, 1), 0)).astype(f32)
        place_k = lax.broadcasted_iota(jnp.int32, (128, width), 1).astype(f32)
        first_one = count(0, 0, 0)
        first_two = length - count(2 * CHIPS - 1, 0, 2) if source == CHIPS - 1 else None
        allowed = (place_k >= first_seen(place_q, first_one, first_two)) & (place_k <= place_q)
        scores = jnp.where(allowed, scores, -1e30)
        weights = jnp.exp(scores - jnp.max(scores, axis=1, keepdims=True))
        probs = (weights / jnp.sum(weights, axis=1, keepdims=True)).astype(LOW)
        r.probs[source, :, 0:width] = probs
        attended = dot(probs, both)
        r.accum[source] = attended
        r.a_out[source] = jnp.where(left64, turned(attended[:64]), attended[64:]).astype(LOW)
        a_spread.start(source)

    for source in range(CHIPS):
        slot = r.mem_in.at[core, source]
        links.local(slot, slot, mem_base + source).wait()
    mem_pair = Pair(links, r.mem_in.at[core], r.mem_in.at[core])
    mem_pair.start()
    mem_pair.wait()
    for source in range(CHIPS):
        for side in range(2):
            found = r.mem_in[side, source].astype(f32)
            at = (2 * source + side) * 8
            r.mem_f32[at : at + 8, 0:256] = found[0:8]
            r.mem_f32[at : at + 8, 256:512] = found[8:16]
    mem_all = r.mem_f32[...].astype(LOW)
    r.mem_rows[row] = mem_all
    mem_x_sem = links.take(1)
    mem_x = links.copy(r.mem_rows.at[row], r.mem_rows.at[row], place.moved("x", 1)[1], mem_x_sem, mem_x_sem)
    mem_x.start()
    r.mem_k[...] = dot(mem_all, weight("cross_key")[...]).astype(LOW)
    r.mem_v[...] = dot(mem_all, weight("cross_value")[...]).astype(LOW)

    for source in range(CHIPS):
        a_spread.wait_from(source)
    for pair in range(4):
        block = unfold_pair(r.a_in[2 * pair].astype(f32), r.a_in[2 * pair + 1].astype(f32))
        r.left_attended[own_rows, 128 * pair : 128 * pair + 128] = block.astype(LOW)
    give_left("attended")
    gains = types.SimpleNamespace(**{name: getattr(r, name)[...].reshape(1, MODEL) for name in VECTORS})
    attended = r.left_attended[own_rows, :]
    first, unit_one, scale_one = normed(
        tokens.astype(f32) + dot(attended, weight("self_out")[...]), gains.gain_one, gains.shift_one
    )
    first_low = first.astype(LOW)
    r.left_first[own_rows, :] = first_low
    give_left("first")
    r.cross_q[...] = (dot(first_low, weight("cross_query")[...]) * scale).astype(LOW)

    place_q = (seq * TOKENS + lax.broadcasted_iota(jnp.int32, (128, 1), 0)).astype(f32)
    first_one, first_two = count(0, 0, 0), length - count(2 * CHIPS - 1, 0, 2)
    mem_one, mem_two = count(0, 1, 0), TOKENS - count(2 * CHIPS - 1, 1, 2)
    mem_one = mem_one - (TOKENS - 8)
    id_q = jnp.where(place_q < first_one, 0.0, jnp.where(place_q < first_two, 1.0, 2.0))
    place_m = lax.broadcasted_iota(jnp.int32, (1, 128), 1).astype(f32)
    id_m = jnp.where(place_m < mem_one, 0.0, jnp.where(place_m < mem_two, 1.0, 2.0))
    seen = id_q == id_m
    seen = jnp.concatenate([seen.astype(f32), seen.astype(f32)], axis=0) > 0.5

    def stacked(block):
        zero = jnp.zeros_like(block)
        return jnp.concatenate([jnp.where(left128, block, zero), jnp.where(left128, zero, block)], axis=0)

    for pair in range(4):
        lanes = slice(128 * pair, 128 * pair + 128)
        scores = dot_rows(stacked(r.cross_q[:, lanes]), r.mem_k[:, lanes])
        scores = jnp.where(seen, scores, -1e30)
        weights = jnp.exp(scores - jnp.max(scores, axis=1, keepdims=True))
        probs = weights / jnp.sum(weights, axis=1, keepdims=True)
        r.cross_p[256 * pair : 256 * pair + 256] = probs
        mixed = dot(probs.astype(LOW), r.mem_v[:, lanes])
        r.left_crossed[own_rows, lanes] = jnp.where(left128, mixed[:128], mixed[128:]).astype(LOW)
    give_left("crossed")
    crossed = r.left_crossed[own_rows, :]
    second, unit_two, scale_two = normed(first + dot(crossed, weight("cross_out")[...]), gains.gain_two, gains.shift_two)
    second_low = second.astype(LOW)
    r.left_second[own_rows, :] = second_low
    give_left("second")
    third = second
    for number in range(4):
        wide = slice(512 * number, 512 * number + 512)
        gate = dot(second_low, weight("expand_weight")[:, wide])
        sigma = 1.0 / (1.0 + jnp.exp(-gate))
        hidden = (gate * sigma).astype(LOW)
        r.gate[:, wide] = sigma * (1.0 + gate * (1.0 - sigma))
        r.left_hidden[own_rows, wide] = hidden
        third = third + dot(hidden, weight("reduce_weight")[wide, :])
    give_left("hidden")
    result, unit_three, scale_three = normed(third, gains.gain_three, gains.shift_three)
    r.layer_output[...] = result.astype(LOW)

    part = r.part
    pieces, landing_at, start = [], 0, 0
    for size in PIECES:
        pieces.append(Summed(links, part, r.landing, r.done, start, size, landing_at))
        landing_at, start = pieces[-1].landing_end, start + size
    begun = []

    def begin(number):
        pieces[number].begin()
        begun.append(number)

    d_third, d_gain_three, d_shift_three = normed_back(
        r.output_cotangent[...].astype(f32), unit_three, scale_three, gains.gain_three
    )
    d_branch = d_third.astype(LOW)
    r.full_d_branch[...] = d_branch
    give_right("d_branch")
    d_second = d_third
    for number in range(4):
        wide = slice(512 * number, 512 * number + 512)
        d_gate = (dot_rows(d_branch, weight("reduce_weight")[wide, :]) * r.gate[:, wide]).astype(LOW)
        r.full_d_gate[:, wide] = d_gate
        d_second = d_second + dot_rows(d_gate, weight("expand_weight")[:, wide])
    give_right("d_gate")

    def outer(at, left_name, columns, right_name, right_columns):
        made = dot_tokens(left(left_name)[:, columns], right(right_name)[:, right_columns])
        part[at : at + 512] = made.astype(LOW)

    every, short = slice(0, 512), slice(0, 256)
    for number in range(4):
        outer(AT.reduce + 512 * number, "hidden", slice(512 * number, 512 * number + 512), "d_branch", short)
        if number % 2 == 1:
            begin(number // 2)
    for number in range(4):
        outer(AT.expand + 512 * number, "second", every, "d_gate", slice(256 * number, 256 * number + 256))
        if number % 2 == 1:
            begin(2 + number // 2)
    d_mid, d_gain_two, d_shift_two = normed_back(d_second, unit_two, scale_two, gains.gain_two)
    d_cross = d_mid.astype(LOW)
    r.full_d_cross[...] = d_cross
    give_right("d_cross")
    r.crossed_d[...] = dot_rows(d_cross, weight("cross_out")[...]).astype(LOW)
    for pair in range(4):
        lanes = slice(128 * pair, 128 * pair + 128)
        probs = r.cross_p[256 * pair : 256 * pair + 256]
        d_out = stacked(r.crossed_d[:, lanes])
        d_probs = dot_rows(d_out, r.mem_v[:, lanes])
        delta = jnp.sum(probs * d_probs, axis=1, keepdims=True)
        d_scores = (probs * (d_probs - delta)).astype(LOW)
        mixed = dot(d_scores, r.mem_k[:, lanes]) * scale
        r.full_d_cross_q[:, lanes] = jnp.where(left128, mixed[:128], mixed[128:]).astype(LOW)
        r.d_mem[0, :, lanes] = dot_tokens(d_scores, stacked(r.cross_q[:, lanes]))
        r.d_mem[1, :, lanes] = dot_tokens(probs.astype(LOW), d_out)
    give_right("d_cross_q")
    mine = pl.ds(pl.multiple_of(core * 256, 256), 256)
    others = pl.ds(pl.multiple_of((1 - core) * 256, 256), 256)
    r.d_mem_out[...] = r.d_mem[:, :, others].astype(LOW)
    mem_grads = Pair(links, r.d_mem_out, r.d_mem_pair)
    mem_grads.start()
    d_first = d_mid + dot_rows(r.full_d_cross_q[...], weight("cross_query")[...])
    d_start, d_gain_one, d_shift_one = normed_back(d_first, unit_one, scale_one, gains.gain_one)
    r.d_start[...] = d_start
    d_self = d_start.astype(LOW)
    r.full_d_self[...] = d_self
    give_right("d_self")
    d_attended = dot_rows(d_self, weight("self_out")[...])
    for pair in range(4):
        even, odd = fold_pair(d_attended[:, 128 * pair : 128 * pair + 128])
        r.da_out[2 * pair] = even.astype(LOW)
        r.da_out[2 * pair + 1] = odd.astype(LOW)
    da_spread = Spread(links, r.da_out, r.da_in)
    da_spread.start_all()
    made = [d_gain_one, d_shift_one, d_gain_two, d_shift_two, d_gain_three, d_shift_three]
    r.rows_held[...] = jnp.concatenate(made + [jnp.zeros((2, MODEL), f32)], axis=0)
    norm_rows = Rows(links, r.rows_held, r.rows_in)
    norm_rows.begin()

    outer(AT.cross_out, "crossed", every, "d_cross", short)
    mem_grads.wait()
    mem_at = AT.memory
    for side in range(2):
        total = r.d_mem[side, :, mine] + r.d_mem_pair[side].astype(f32)
        part[rows_at(mem_at + row * 256 + side * 128, 128)] = total.astype(LOW)
        part[rows_at(mem_at + (1 - row) * 256 + side * 128, 128)] = jnp.zeros((128, 256), LOW)
    begin(4)
    outer(AT.cross_query, "first", every, "d_cross_q", short)
    outer(AT.self_out, "attended", every, "d_self", short)
    begin(5)

    waiting = {number: 0 for number in range(len(pieces))}
    row_events = [0]

    def advance(count):
        for _ in range(count):
            ready = [number for number in begun if waiting[number] < 7]
            if not ready:
                return
            number = min(ready, key=lambda item: (item + 1.5 * waiting[item], item))
            pieces[number].advance(waiting[number])
            waiting[number] += 1

    def advance_rows():
        norm_rows.advance(row_events[0])
        row_events[0] += 1

    advance(2)
    dq_spread = Spread(links, r.dq_out, r.dq_in)
    dkv_spread = Spread(links, r.dkv_out, r.dkv_in)
    dkv_pairs = {}

    def dkv_finish(source):
        dkv_pairs[source].wait()
        r.dkv_out[source] = (r.dkv[2 * source + core] + r.dkv_pair[source]).astype(LOW)
        dkv_spread.start(source)

    for source in reversed(range(CHIPS)):
        da_spread.wait_from(source)
        width = 256 * (source + 1)
        folded = r.da_in[source].astype(f32)
        left64 = left_lanes(64)
        d_out = jnp.concatenate([jnp.where(left64, 0.0, turned(folded)), jnp.where(left64, 0.0, folded)], axis=0)
        delta = jnp.sum(d_out * r.accum[source], axis=1, keepdims=True)
        d_out = d_out.astype(LOW)
        both = r.kv_in[0 : 2 * source + 2, 0:128].reshape(width, 128)
        d_probs = dot_rows(d_out, both)
        probs = r.probs[source, :, 0:width]
        d_scores = (probs.astype(f32) * (d_probs - delta)).astype(LOW)
        d_query = dot(d_scores, both) * scale
        r.dq_out[source] = jnp.where(left64, d_query[:64], turned(d_query[64:])).astype(LOW)
        dq_spread.start(source)
        d_both = dot_tokens(
            jnp.concatenate([d_scores, probs], axis=0), jnp.concatenate([r.q_pad[source], d_out], axis=0)
        ).reshape(2 * source + 2, 128, 128)
        if source == CHIPS - 1:
            r.dkv[...] = d_both
        else:
            r.dkv[0 : 2 * source + 2] = r.dkv[0 : 2 * source + 2] + d_both
        dkv_pairs[source] = Pair(links, r.dkv.at[2 * source + 1 - core], r.dkv_pair.at[source])
        dkv_pairs[source].start()
        if source + 1 < CHIPS:
            dkv_finish(source + 1)
        advance(2)
        if source % 2 == 0:
            advance_rows()
    dkv_finish(0)

    for source in range(CHIPS):
        dq_spread.wait_from(source)
        dkv_spread.wait_from(source)
    for pair in range(4):
        lanes = slice(128 * pair, 128 * pair + 128)
        block = unfold_pair(r.dq_in[2 * pair].astype(f32), r.dq_in[2 * pair + 1].astype(f32))
        r.full_d_q[:, lanes] = block.astype(LOW)
        even, odd = r.dkv_in[2 * pair].astype(f32), r.dkv_in[2 * pair + 1].astype(f32)
        r.full_d_k[:, lanes] = jnp.where(left128, even, turned(odd)).astype(LOW)
        r.full_d_v[:, lanes] = jnp.where(left128, turned(even), odd).astype(LOW)
    for name in ("d_q", "d_k", "d_v"):
        give_right(name)
    for name, kind in (("d_q", "self_query"), ("d_k", "self_key"), ("d_v", "self_value")):
        outer(getattr(AT, kind), "states", every, name, short)
    begin(6)
    grad = r.d_start[...]
    for name, kind in (("d_q", "self_query"), ("d_k", "self_key"), ("d_v", "self_value")):
        grad = grad + dot_rows(getattr(r, "full_" + name)[...], weight(kind)[...])
    r.states_grad[...] = grad

    done, sums = r.done, r.sums
    mem_x.wait()
    out_base = links.take(len(pieces) + 1)
    outs = []

    def put(start, size):
        rows = pl.ds(start, size)
        copy = links.local(done.at[:, rows], sums.at[:, rows], out_base + len(outs))
        copy.start()
        outs.append(copy)

    written = set()

    def flush():
        for number, piece in enumerate(pieces):
            if waiting[number] == 7 and number not in written:
                put(piece.start, piece.size)
                written.add(number)

    extra = []

    def memory_sums():
        mems = r.mem_rows[...].reshape(2 * TOKENS, MODEL)
        for side, kind in ((0, "cross_key"), (1, "cross_value")):
            grads = [done[core, mem_at + 256 * number + 128 * side : mem_at + 256 * number + 128 * side + 128] for number in range(2)]
            made = dot_tokens(mems, jnp.concatenate(grads, axis=0))
            done[core, getattr(AT, kind) : getattr(AT, kind) + 512] = made.astype(LOW)
        mine = done.at[core, pl.ds(SUMMED_ROWS, DONE_ROWS - SUMMED_ROWS)]
        extra.append(Pair(links, mine, mine))
        extra[0].start()

    def memory_out():
        grads = []
        for side in range(2):
            rows = rows_at(mem_at + row * 256 + side * 128 + chip * 16, 16)
            grads.append(jnp.concatenate([done[0, rows], done[1, rows]], axis=1))
        both = dot_rows(grads[0], weight("cross_key")[...]) + dot_rows(grads[1], weight("cross_value")[...])
        r.memory_grad[...] = jnp.where(core == 0, both[0:8], both[8:16])
        extra[0].wait()
        put(SUMMED_ROWS, DONE_ROWS - SUMMED_ROWS)

    while any(count < 7 for count in waiting.values()):
        before = waiting[4]
        advance(1)
        if before < 6 and waiting[4] == 6:
            memory_sums()
        if before < 7 and waiting[4] == 7:
            memory_out()
        flush()
    r.rows[...] = r.rows_held[...]
    for hop in range(1, CHIPS):
        kv_copy(hop).wait_send()
        mem_copy(hop).wait_send()
    q_spread.end_all()
    da_spread.end_all()
    for source in range(CHIPS):
        a_spread.end(source)
        dq_spread.end(source)
        dkv_spread.end(source)
    for copy in outs:
        copy.wait()


def finish_kernel(rows, sums, *refs):
    names = tuple(WEIGHTS) + VECTORS
    out = dict(zip(names, refs))
    low, wide, fetch, store = refs[len(names) :]
    blocks = []
    for core in range(2):
        for number in range(4):
            blocks.append((core, AT.reduce + 512 * number, "reduce_weight", 512 * number, 256 * core))
            blocks.append((core, AT.expand + 512 * number, "expand_weight", 0, 1024 * core + 256 * number))
        for name in WEIGHTS:
            if hasattr(AT, name):
                blocks.append((core, getattr(AT, name), name, 0, 256 * core))
    reads, writes = [], []
    for number, (core, at, name, down, along) in enumerate(blocks):
        reads.append(pltpu.make_async_copy(sums.at[core, pl.ds(at, 512)], low.at[number], fetch.at[number]))
        there = out[name].at[pl.ds(down, 512), pl.ds(along, 256)]
        writes.append(pltpu.make_async_copy(wide.at[number], there, store.at[number]))
    for read in reads:
        read.start()
    for number, name in enumerate(VECTORS):
        out[name][...] = rows[number, :]
    for number, (read, write) in enumerate(zip(reads, writes)):
        read.wait()
        wide[number] = low[number].astype(jnp.float32)
        write.start()
    for write in writes:
        write.wait()


def fast_body(*given):
    names = tuple(inspect.signature(body).parameters)
    arrays = dict(zip(names, given))
    for name in ("states", "memory", "output_cotangent"):
        arrays[name] = arrays[name][0]
    vmem = pl.BlockSpec(memory_space=pltpu.VMEM)
    hbm = pl.BlockSpec(memory_space=pl.ANY)
    f32 = jnp.float32
    semaphores = pltpu.SemaphoreType.DMA((SEMAPHORES,))
    layer_output, states_grad, memory_grad, rows, sums = pl.pallas_call(
        layer_kernel,
        out_shape=(
            jax.ShapeDtypeStruct((TOKENS, MODEL), LOW),
            jax.ShapeDtypeStruct((TOKENS, MODEL), f32),
            jax.ShapeDtypeStruct((8, MODEL), f32),
            jax.ShapeDtypeStruct((SLOTS, MODEL), f32),
            jax.ShapeDtypeStruct((2, DONE_ROWS, 256), LOW),
        ),
        in_specs=[vmem] * len(GIVEN) + [hbm] * len(WEIGHTS),
        out_specs=(vmem, vmem, vmem, vmem, hbm),
        scratch_shapes=[pltpu.VMEM(shape, kind) for shape, kind in scratch_of().values()]
        + [semaphores, semaphores, pltpu.SemaphoreType.DMA((len(WEIGHTS),))],
        compiler_params=pltpu.CompilerParams(collective_id=0, has_side_effects=True, vmem_limit_bytes=60 << 20),
    )(*[arrays[name] for name in GIVEN], *[arrays[name] for name in WEIGHTS])
    blocks = 32
    made = pl.pallas_call(
        finish_kernel,
        out_shape=tuple(jax.ShapeDtypeStruct(shape, f32) for shape in WEIGHTS.values())
        + tuple(jax.ShapeDtypeStruct((MODEL,), f32) for _ in VECTORS),
        in_specs=[vmem, hbm],
        out_specs=tuple([hbm] * len(WEIGHTS) + [vmem] * len(VECTORS)),
        scratch_shapes=[
            pltpu.VMEM((blocks, 512, 256), LOW),
            pltpu.VMEM((blocks, 512, 256), f32),
            pltpu.SemaphoreType.DMA((blocks,)),
            pltpu.SemaphoreType.DMA((blocks,)),
        ],
        compiler_params=pltpu.CompilerParams(vmem_limit_bytes=48 << 20),
    )(rows, sums)
    grads = dict(zip(tuple(WEIGHTS) + VECTORS, made))
    return (layer_output[None], states_grad[None], memory_grad[None]) + tuple(grads[name] for name in names[4:-1])


def solution(mesh):
    def either(*given):
        shapes = [given[0].shape, given[1].shape, given[16].shape]
        fits = shapes == [(1, TOKENS, MODEL), (1, 8, MODEL), (MODEL, HIDDEN)]
        fits = fits and dict(mesh.shape) == {ROWS: EXTENT["x"], SEQ: 2 * CHIPS}
        return (fast_body if fits else body)(*given)

    return jax.shard_map(
        either,
        mesh=mesh,
        in_specs=(
            P(ROWS, SEQ, None),
            P(ROWS, SEQ, None),
            P(ROWS, SEQ),
            P(ROWS, SEQ),
            P(),
            P(),
            P(),
            P(),
            P(),
            P(),
            P(),
            P(),
            P(),
            P(),
            P(),
            P(),
            P(),
            P(),
            P(),
            P(),
            P(ROWS, SEQ, None),
        ),
        out_specs=(
            P(ROWS, SEQ, None),
            P(ROWS, SEQ, None),
            P(ROWS, SEQ, None),
            P(),
            P(),
            P(),
            P(),
            P(),
            P(),
            P(),
            P(),
            P(),
            P(),
            P(),
            P(),
            P(),
            P(),
            P(),
            P(),
        ),
        check_vma=False,
    )
```
